128 devices in a mesh: section: 2 (over z_hi), mp: 8 (over y, core), dp: 8 (over x, z_lo).
Axes of the slice: x: 4, y: 4, z: 4 (z_hi: 2, z_lo: 2; z = z_hi * 2 + z_lo), core: 2. Of those that a mesh axis runs over, the one named last changes fastest.
Arguments:
- context: bfloat16 [2, 2048, 6144], P('section', 'dp', 'mp'), may hold values from -6 to 6
- residual: bfloat16 [2, 2048, 8192], P('section', ('dp', 'mp')), may hold values from -6 to 6
- out_weight: bfloat16 [2, 6144, 8192], P('section', 'mp', 'dp'), may hold values from -0.078125 to 0.078125
- ln_gain: float32 [2, 8192], P('section'), may hold values from 0.1 to 1.9
- ln_bias: float32 [2, 8192], P('section'), may hold values from -0.5 to 0.5
- out_grad: bfloat16 [2, 2048, 8192], P('section', ('dp', 'mp')), may hold values from -16 to 16
Outputs:
- normed: bfloat16 [2, 2048, 8192], P('section', ('dp', 'mp'))
- grad_residual: bfloat16 [2, 2048, 8192], P('section', ('dp', 'mp'))
- grad_context: bfloat16 [2, 2048, 6144], P('section', 'dp', 'mp')
- grad_weight: float32 [2, 6144, 8192], P('section', 'mp', 'dp')
- gain_grad: float32 [2, 8192], P('section')
- bias_grad: float32 [2, 8192], P('section')
The draws below stay inside these ranges and needn't reach their ends.
All inputs are finite; a program needn't handle non-finite values.
Results may differ from the reference program's by a relative error of at most 0.017.
Values may be sent and summed in bfloat16 or wider, within the bound.
No kernel may reach another device: no remote copies, remote signals or barrier semaphores. Data moves between devices by JAX's collectives and lax.ppermute only.
A program may use at most 128 MiB of HBM per device.

```python
import jax
import jax.numpy as jnp
from jax import lax

D = 8192
ATT_WIDTH = 6144
TOK_DEV = 256
TOKENS = 2048
N_SECTION = 2


def with_spikes(entries, key, source, target, parts, factor):
    owner, partner = [(jnp.arange(entries.shape[dim]) // (entries.shape[dim] // parts)).reshape([-1 if axis == dim else 1 for axis in range(entries.ndim)]) for dim in (source, target)]
    chosen = jax.random.permutation(key, parts)[partner]
    strong = (owner == chosen) | (owner == (partner + parts // 2) % parts)
    return jnp.where(strong, factor * entries, entries)


def level_of(stream_key, dims, split, least, high):
    loudness, own = 1.0, jax.random.fold_in(stream_key, 6)
    for position, parts in split:
        steps = jnp.exp(jax.random.uniform(jax.random.fold_in(own, position), (parts,), jnp.float32, least / len(split), high / len(split)))
        loudness = loudness * jnp.repeat(steps, dims[position] // parts).reshape([-1 if axis == position else 1 for axis in range(len(dims))])
    return loudness


def centred(own_key, dims, scale, most, shards=(), held_as=jnp.bfloat16):
    values = scale * jax.random.normal(own_key, dims, jnp.float32)
    if shards:
        values = values * level_of(own_key, dims, shards, -0.22, 0.18)
    return jnp.clip(values, -most, most).astype(held_as)


def heavy_noise(own_key, extent, deviation, limit, pieces, heavy, kind=jnp.bfloat16):
    array = deviation * jax.random.normal(own_key, extent, jnp.float32)
    if pieces:
        array = array * level_of(own_key, extent, pieces, -0.22, 0.18)
    return jnp.clip(with_spikes(array, jax.random.fold_in(own_key, 3), *heavy), -limit, limit).astype(kind)


def setup_inputs(seed: int = 0) -> dict:
    arg_keys = jax.random.split(jax.random.key(seed), 7)
    context = centred(arg_keys[0], (2, TOKENS, ATT_WIDTH), 1.0, 6.0, ((0, 2), (1, 8), (2, 8)))
    residual = centred(arg_keys[1], (2, TOKENS, D), 1.0, 6.0, ((0, 2), (1, 64)))
    out_weight = centred(arg_keys[2], (2, ATT_WIDTH, D), ATT_WIDTH ** -0.5, 0.078125, ((0, 2), (1, 8), (2, 8)))
    ln_gain = jnp.clip(1.0 + 0.18 * jax.random.normal(arg_keys[3], (2, D), jnp.float32), 0.1, 1.9)
    ln_bias = jnp.clip(jax.random.uniform(arg_keys[4], (2, D), jnp.float32, -0.5, 0.5) * level_of(arg_keys[4], (2, D), ((0, 2),), -0.4, 0.0), -0.5, 0.5)
    out_grad = heavy_noise(arg_keys[5], (2, TOKENS, D), 1.0, 16.0, ((0, 2), (1, 64)), (1, 2, 64, 4.0))
    return dict(context=context, residual=residual, out_weight=out_weight, ln_gain=ln_gain, ln_bias=ln_bias, out_grad=out_grad)


EPSILON = 1e-05

def normalize(values, gain_row, bias_row):
    center = lax.optimization_barrier(jnp.mean(values, axis=-1, keepdims=True))
    shifted = values - center
    spread = lax.optimization_barrier(jnp.mean(shifted * shifted, axis=-1, keepdims=True))
    scaled = lax.rsqrt(spread + EPSILON)
    standard = shifted * scaled
    return (standard, scaled, standard * gain_row + bias_row)

def reference(context, residual, out_weight, ln_gain, ln_bias, out_grad):
    hidden = []
    for member in range(N_SECTION):
        attended = jnp.dot(context[member], out_weight[member], preferred_element_type=jnp.float32)
        hidden.append((residual[member].astype(jnp.float32) + attended).astype(jnp.bfloat16))
    normed = []
    gain_grad = []
    bias_grad = []
    upstream = [None] * N_SECTION
    for member in range(N_SECTION):
        anchor = (member - 1) % N_SECTION
        standard, scaled, result = normalize(hidden[anchor].astype(jnp.float32), ln_gain[member], ln_bias[member])
        normed.append(result.astype(jnp.bfloat16))
        incoming = out_grad[member].astype(jnp.float32)
        weighted = incoming * ln_gain[member]
        returned = scaled * (weighted - lax.optimization_barrier(jnp.mean(weighted, axis=-1, keepdims=True)) - standard * lax.optimization_barrier(jnp.mean(weighted * standard, axis=-1, keepdims=True)))
        upstream[anchor] = returned.astype(jnp.bfloat16)
        gain_grad.append(lax.optimization_barrier(jnp.sum(incoming * standard, axis=0)))
        bias_grad.append(lax.optimization_barrier(jnp.sum(incoming, axis=0)))
    grad_context = []
    grad_weight = []
    for member in range(N_SECTION):
        flowing = upstream[member]
        grad_context.append(lax.dot_general(flowing, out_weight[member], (((1,), (1,)), ((), ())), preferred_element_type=jnp.float32).astype(jnp.bfloat16))
        running = jnp.zeros((ATT_WIDTH, D), jnp.float32)
        for dp_block in range(TOKENS // TOK_DEV):
            context_rows = context[member, dp_block * TOK_DEV:(dp_block + 1) * TOK_DEV]
            flowing_rows = flowing[dp_block * TOK_DEV:(dp_block + 1) * TOK_DEV]
            partial_term = lax.dot_general(context_rows, flowing_rows, (((0,), (0,)), ((), ())), preferred_element_type=jnp.float32)
            rounded = lax.optimization_barrier(partial_term.astype(jnp.bfloat16)).astype(jnp.float32)
            running = running + rounded
        grad_weight.append(running)
    return (jnp.stack(normed), jnp.stack(upstream), jnp.stack(grad_context), jnp.stack(grad_weight), jnp.stack(gain_grad), jnp.stack(bias_grad))
```

```python
import jax
import jax.numpy as jnp
from jax import lax
from jax.sharding import PartitionSpec as P

EPSILON = 1e-05
WIDTH = 8192
BF = jnp.bfloat16
F32 = jnp.float32


def over_core(value):
    return lax.ppermute(value, "mp", [(i, i ^ 1) for i in range(8)])


def over_y(value, steps):
    return lax.ppermute(value, "mp", [(i, (i + 2 * steps) % 8) for i in range(8)])


def over_dp(value, steps, flip):
    return lax.ppermute(
        value, "dp", [(j, 2 * (((j >> 1) + steps) % 4) + ((j & 1) ^ flip)) for j in range(8)]
    )


def over_section(value, steps):
    return lax.ppermute(value, "section", [(s, (s + steps) % 2) for s in range(2)])


FIRST = ((0, 0), (0, 1), (1, 0), (3, 0))
SECOND = ((2, 0), (1, 1), (3, 1), (2, 1))
ORDER = FIRST + SECOND
NATURAL = tuple((k, f) for k in range(4) for f in range(2))


def aligned(stats, steps, flip):
    blocks = stats.reshape(4, 8, 32)
    places = [ORDER.index(((k - steps) % 4, f ^ flip)) for k, f in ORDER]
    return jnp.stack([blocks[:, p] for p in places], axis=1).reshape(4, 256)


def merged(parts):
    count = len(parts)
    width = parts[0][1]
    mean = sum(p[0][0] for p in parts) / count
    squares = sum(p[0][1] + width * jnp.square(p[0][0] - mean) for p in parts)
    total = sum(p[0][2] for p in parts)
    cross = sum(p[0][3] + (p[0][0] - mean) * p[0][2] for p in parts)
    return (jnp.stack([mean, squares, total, cross]), width * count)


def shards(context, residual, out_weight, ln_gain, ln_bias, out_grad):
    mp, dp = lax.axis_index("mp"), lax.axis_index("dp")
    y, core = mp // 2, mp % 2
    x, z = dp // 2, dp % 2

    blocks = context[0].reshape(4, 2, 32, 768)
    by_y = [lax.dynamic_index_in_dim(blocks, (y - k) % 4, 0, False) for k in range(4)]
    mine = jnp.stack([lax.dynamic_index_in_dim(b, core, 0, False) for b in by_y])
    theirs = jnp.stack([lax.dynamic_index_in_dim(b, 1 - core, 0, False) for b in by_y])
    half = jnp.concatenate([mine, over_core(theirs)], axis=-1)
    weight_own = out_weight[0]
    weight_other = over_core(weight_own)
    columns = jnp.concatenate(
        [
            lax.dynamic_slice_in_dim(ln_gain, dp * 1024, 1024, 1),
            lax.dynamic_slice_in_dim(ln_bias, dp * 1024, 1024, 1),
        ],
        axis=0,
    )
    columns = over_section(columns, -1)
    gain, bias = columns[0], columns[1]
    cotangent = over_section(out_grad[0], -1)

    got = {(0, 0): half}
    got[(0, 1)] = over_dp(half, 0, 1)
    for k in (1, 3, 2):
        got[(k, 0)] = over_dp(half, k, 0)
    for k in (1, 3):
        got[(k, 1)] = over_dp(got[(0, 1)], k, 0)
    got[(2, 1)] = over_dp(got[(2, 0)], 0, 1)

    pair = jnp.stack([residual[0], cotangent]).reshape(2, 32, 8, 1024)
    turned = {}
    for k, f in ORDER:
        block = lax.dynamic_index_in_dim(pair, 2 * ((x + k) % 4) + (z ^ f), 2, False)
        turned[(k, f)] = over_dp(block, k, f) if (k, f) != (0, 0) else block
    turned = jnp.stack([turned[r] for r in ORDER], axis=1)
    stream, incoming = turned[0].astype(F32), turned[1].astype(F32)

    weights = jnp.concatenate([weight_own, weight_other], axis=0)
    attended, tokens = [], []
    for group in (FIRST, SECOND):
        rows = jnp.stack([got[r] for r in group], axis=1)
        tokens.append(rows)
        part = jnp.dot(rows.reshape(512, 1536), weights, preferred_element_type=F32).reshape(4, 4, 32, 1024)
        total = part[0]
        for k in (1, 3, 2):
            total = total + over_y(part[k].astype(BF), -k).astype(F32)
        attended.append(total)
    hidden = (stream + jnp.concatenate(attended, axis=0)).astype(BF).astype(F32)

    weighted = incoming * gain
    mean_here = jnp.mean(hidden, axis=-1)
    shifted = hidden - mean_here[..., None]
    here = jnp.stack(
        [
            mean_here,
            jnp.sum(shifted * shifted, axis=-1),
            jnp.sum(weighted, axis=-1),
            jnp.sum(weighted * shifted, axis=-1),
        ]
    ).reshape(4, 256)
    stats = merged([(here, 1024), (aligned(over_dp(here, 0, 1), 0, 1), 1024)])
    stats = merged([stats] + [(aligned(over_dp(stats[0], k, 0), k, 0), stats[1]) for k in (1, 2, 3)])[0]
    center, squares, total, cross = (s.reshape(8, 32, 1) for s in stats)
    scaled = lax.rsqrt(squares / WIDTH + EPSILON)
    standard = (hidden - center) * scaled
    returned = (scaled * (weighted - total / WIDTH - standard * (cross * scaled / WIDTH))).astype(BF)
    normed = (standard * gain + bias).astype(BF)

    flowing = [returned] + [over_y(returned, k) for k in (1, 2, 3)]
    outgoing = jnp.stack([normed, returned], axis=1)
    back = {}
    for place, (k, f) in enumerate(ORDER):
        block = outgoing[place]
        back[(k, f)] = over_dp(block, -k, f) if (k, f) != (0, 0) else block
    back = jnp.stack([back[r] for r in NATURAL])
    rows_back = jnp.stack(
        [
            lax.dynamic_index_in_dim(back, 2 * ((b // 2 - x) % 4) + ((b % 2) ^ z), 0, False)
            for b in range(8)
        ],
        axis=2,
    ).reshape(2, 32, 8192)
    upstream = rows_back[1]
    normed_rows = over_section(rows_back[0], 1)

    sums = jnp.stack([jnp.sum(incoming * standard, axis=(0, 1)), jnp.sum(incoming, axis=(0, 1))])
    sums = sums + over_core(sums)
    sums = sums + sum(over_y(sums, k) for k in (1, 2, 3))
    sums = over_section(sums, 1)
    sums = jnp.stack([sums, over_dp(sums, 0, 1)])
    sums = jnp.stack([sums] + [over_dp(sums, k, 0) for k in (1, 2, 3)])
    flat = sums.reshape(8, 2, 1024)
    whole = jnp.stack(
        [
            lax.dynamic_index_in_dim(flat, 2 * ((x - b // 2) % 4) + ((b % 2) ^ z), 0, False)
            for b in range(8)
        ],
        axis=1,
    ).reshape(2, 8192)

    terms = []
    for rows in flowing:
        terms.append(
            lax.dot_general(
                rows.reshape(256, 1024), weights, (((1,), (1,)), ((), ())), preferred_element_type=F32
            ).reshape(8, 32, 1536)
        )
    terms = jnp.stack(terms, axis=1)
    term = {r: terms[place] for place, r in enumerate(ORDER)}
    crossing = over_dp(term[(2, 1)].astype(BF), 0, 1).astype(F32)
    far = over_dp((term[(2, 0)] + crossing).astype(BF), -2, 0).astype(F32)
    other = term[(0, 1)]
    for k in (1, 3):
        other = other + over_dp(term[(k, 1)].astype(BF), -k, 0).astype(F32)
    context_sum = term[(0, 0)] + far
    for k in (1, 3):
        context_sum = context_sum + over_dp(term[(k, 0)].astype(BF), -k, 0).astype(F32)
    context_sum = context_sum + over_dp(other.astype(BF), 0, 1).astype(F32)
    context_sum = context_sum.astype(BF)
    kept, given = context_sum[..., :768], over_core(context_sum[..., 768:])
    both = jnp.stack([kept, given], axis=1)
    both = jnp.stack(
        [lax.dynamic_index_in_dim(both, (y - b) % 4, 0, False) for b in range(4)]
    )
    grad_context = jnp.where(core == 0, both, both[:, ::-1]).reshape(256, 768)

    spread = jnp.stack(flowing)
    weight_sum = sum(
        lax.dot_general(
            tokens[g], spread[:, 4 * g : 4 * g + 4], (((0, 1, 2), (0, 1, 2)), ((), ())), preferred_element_type=F32
        )
        for g in (0, 1)
    )
    grad_weight = weight_sum[:768] + over_core(weight_sum[768:].astype(BF)).astype(F32)
    return (
        normed_rows[None],
        upstream[None],
        grad_context[None],
        grad_weight[None],
        whole[0][None],
        whole[1][None],
    )


def solution(mesh):
    return jax.shard_map(
        shards,
        mesh=mesh,
        in_specs=(
            P("section", "dp", "mp"),
            P("section", ("dp", "mp"), None),
            P("section", "mp", "dp"),
            P("section", None),
            P("section", None),
            P("section", ("dp", "mp"), None),
        ),
        out_specs=(
            P("section", ("dp", "mp"), None),
            P("section", ("dp", "mp"), None),
            P("section", "dp", "mp"),
            P("section", "mp", "dp"),
            P("section", None),
            P("section", None),
        ),
        check_vma=False,
    )
```

```python
import jax
import jax.numpy as jnp
from jax import lax
from jax.experimental import pallas as pl
from jax.experimental.pallas import tpu as pltpu
from jax.sharding import PartitionSpec as P

EPSILON = 1e-05
WIDTH = 8192
BF = jnp.bfloat16
F32 = jnp.float32


def over_core(value):
    return lax.ppermute(value, "mp", [(i, i ^ 1) for i in range(8)])


def over_y(value, steps):
    return lax.ppermute(value, "mp", [(i, (i + 2 * steps) % 8) for i in range(8)])


def over_dp(value, steps, flip):
    return lax.ppermute(
        value, "dp", [(j, 2 * (((j >> 1) + steps) % 4) + ((j & 1) ^ flip)) for j in range(8)]
    )


def over_section(value, steps):
    return lax.ppermute(value, "section", [(s, (s + steps) % 2) for s in range(2)])


FIRST = ((0, 0), (0, 1), (1, 0), (3, 0))
SECOND = ((2, 0), (1, 1), (3, 1), (2, 1))
ORDER = FIRST + SECOND
NATURAL = tuple((k, f) for k in range(4) for f in range(2))


LANES = 128


def hidden_kernel(first, first_1, first_2, first_3, second, second_1, second_2, second_3, own, turned_1, turned_2, turned_3, gain, hidden, stats, stats_z):
    lane = lax.broadcasted_iota(jnp.int32, (32, LANES), 1)
    kind, place = lane // 32, lane % 8
    plain = jnp.zeros((32, LANES), F32)
    crossed = jnp.zeros((32, LANES), F32)
    turned = (own, turned_1, turned_2, turned_3)
    for index, (k, f) in enumerate(ORDER):
        group = (first, first_1, first_2, first_3) if index < 4 else (second, second_1, second_2, second_3)
        rows = pl.ds(index % 4 * 32, 32)
        attended = sum(part[rows, :].astype(F32) for part in group)
        value = (turned[k][f, 0].astype(F32) + attended).astype(BF)
        hidden[pl.ds(index * 32, 32), :] = value
        value = value.astype(F32)
        weighted = turned[k][f, 1].astype(F32) * gain[...]
        mean = jnp.sum(value, axis=-1, keepdims=True) * (1.0 / 1024)
        shifted = value - mean
        squares = jnp.sum(shifted * shifted, axis=-1, keepdims=True)
        total = jnp.sum(weighted, axis=-1, keepdims=True)
        cross = jnp.sum(weighted * shifted, axis=-1, keepdims=True)
        both = jnp.where(kind == 0, mean, jnp.where(kind == 1, squares, jnp.where(kind == 2, total, cross)))
        plain = jnp.where(place == 2 * k + f, both, plain)
        crossed = jnp.where(place == 2 * k + 1 - f, both, crossed)
    stats[...] = plain
    stats_z[...] = crossed


def norm_kernel(hidden, own, turned_1, turned_2, turned_3, gain, bias, stats, stats_1, stats_2, stats_3, returned, keep, send):
    sets = [stats[0], stats[1]]
    for k, other in ((1, stats_1), (2, stats_2), (3, stats_3)):
        sets += [pltpu.roll(other[f], 2 * k, 1) for f in (0, 1)]
    added = sum(sets)
    mean = added * 0.125
    squares = pltpu.roll(added, LANES - 32, 1)
    total = pltpu.roll(added, LANES - 64, 1) * (1.0 / WIDTH)
    cross = pltpu.roll(added, LANES - 96, 1)
    for part in sets:
        apart = part - mean
        squares = squares + 1024.0 * apart * apart
        cross = cross + apart * pltpu.roll(part, LANES - 64, 1)
    scaled = lax.rsqrt(squares * (1.0 / WIDTH) + EPSILON)
    cross = cross * scaled * (1.0 / WIDTH)
    turned = (own, turned_1, turned_2, turned_3)
    gain_sum = jnp.zeros((1, 1024), F32)
    bias_sum = jnp.zeros((1, 1024), F32)
    for index, (k, f) in enumerate(ORDER):
        at = 8 + 2 * k + f
        rows = pl.ds(index * 32, 32)
        standard = (hidden[rows, :].astype(F32) - mean[:, at : at + 1]) * scaled[:, at : at + 1]
        incoming = turned[k][f, 1].astype(F32)
        weighted = incoming * gain[...]
        result = scaled[:, at : at + 1] * (weighted - total[:, at : at + 1] - standard * cross[:, at : at + 1])
        result = result.astype(BF)
        target = send if f else keep
        returned[rows, :] = result
        target[k, 32:64, :] = result
        target[k, 0:32, :] = (standard * gain[...] + bias[...]).astype(BF)
        gain_sum = gain_sum + jnp.sum(incoming * standard, axis=0, keepdims=True)
        bias_sum = bias_sum + jnp.sum(incoming, axis=0, keepdims=True)
    row = lax.broadcasted_iota(jnp.int32, (16, 1024), 0)
    lines = jnp.zeros((16, 1024), F32)
    for first, rest in ((0, gain_sum), (3, bias_sum)):
        for place in range(3):
            part = rest.astype(BF).astype(F32)
            lines = jnp.where(row == first + place, part, lines)
            rest = rest - part
    lines = lines.astype(BF)
    for k in range(4):
        keep[k, 64:80, :] = lines
        send[k, 64:80, :] = lines


def called(kernel, results, *operands, flops=20_000_000):
    moved = sum(v.size * v.dtype.itemsize for v in (*operands, *results))
    return pl.pallas_call(
        kernel,
        out_shape=results,
        compiler_params=pltpu.CompilerParams(vmem_limit_bytes=32 * 2**20),
        cost_estimate=pl.CostEstimate(flops=flops, bytes_accessed=moved, transcendentals=4096),
    )(*operands)


def after(value, *others):
    return lax.optimization_barrier((value, *others))[0]


def shards(context, residual, out_weight, ln_gain, ln_bias, out_grad):
    mp, dp = lax.axis_index("mp"), lax.axis_index("dp")
    y, core = mp // 2, mp % 2
    x, z = dp // 2, dp % 2

    blocks = context[0].reshape(4, 2, 32, 768)
    by_y = [lax.dynamic_index_in_dim(blocks, (y - k) % 4, 0, False) for k in range(4)]
    theirs = jnp.stack([lax.dynamic_index_in_dim(b, 1 - core, 0, False) for b in by_y])
    mine = jnp.stack([lax.dynamic_index_in_dim(b, core, 0, False) for b in by_y])
    half = jnp.concatenate([mine, over_core(theirs)], axis=-1)

    got = {(0, 0): half}
    got[(1, 0)] = over_dp(half, 1, 0)
    got[(3, 0)] = over_dp(half, 3, 0)
    got[(0, 1)] = over_dp(half, 0, 1)
    got[(2, 0)] = over_dp(half, 2, 0)
    for k in (1, 3):
        got[(k, 1)] = over_dp(got[(0, 1)], k, 0)
    got[(2, 1)] = over_dp(got[(2, 0)], 0, 1)
    weight_own = out_weight[0]
    weight_other = over_core(after(weight_own, half))
    weights = jnp.concatenate([weight_own, weight_other], axis=0)

    columns = jnp.concatenate(
        [
            lax.dynamic_slice_in_dim(ln_gain, dp * 1024, 1024, 1),
            lax.dynamic_slice_in_dim(ln_bias, dp * 1024, 1024, 1),
        ],
        axis=0,
    )
    cotangent = over_section(after(out_grad[0], got[(0, 1)]), -1)
    columns = over_section(after(columns, got[(2, 0)]), -1)
    gain, bias = columns[:1], columns[1:]

    attended, tokens = [], []
    for group in (FIRST, SECOND):
        rows = jnp.stack([got[r] for r in group], axis=1)
        if attended:
            rows = after(rows, attended[0])
        tokens.append(rows)
        part = jnp.dot(rows.reshape(512, 1536), weights, preferred_element_type=F32).astype(BF)
        part = part.reshape(4, 128, 1024)
        attended += [part[0]] + [over_y(part[k], -k) for k in (1, 3, 2)]

    pair = after(jnp.stack([residual[0], cotangent]), attended[0])
    sides = [
        jnp.stack(
            [
                lax.dynamic_slice_in_dim(pair, (2 * ((x + k) % 4) + side) * 1024, 1024, 2)
                for k in range(4)
            ]
        )
        for side in (z, 1 - z)
    ]
    sides = jnp.stack([sides[0], over_dp(sides[1], 0, 1)], axis=1)
    turned = [sides[0]] + [over_dp(sides[k], k, 0) for k in (1, 2, 3)]

    line = jax.ShapeDtypeStruct((32, LANES), F32)
    rows_here = jax.ShapeDtypeStruct((256, 1024), BF)
    hidden, stats, stats_z = called(
        hidden_kernel, (rows_here, line, line), *attended, *turned, gain
    )
    stats = jnp.stack([stats, over_dp(stats_z, 0, 1)])
    stats = [stats] + [over_dp(stats, k, 0) for k in (1, 2, 3)]
    blocks_out = jax.ShapeDtypeStruct((4, 80, 1024), BF)
    returned, keep, send = called(
        norm_kernel, (rows_here, blocks_out, blocks_out), hidden, *turned, gain, bias, *stats
    )

    returned = returned.reshape(8, 32, 1024)
    flowing = [returned] + [over_y(returned, k) for k in (1, 3, 2)]
    flowing = [flowing[0], flowing[1], flowing[3], flowing[2]]

    by_source = jnp.stack([keep, over_dp(send, 0, 1)], axis=1)
    back = [by_source[0]] + [over_dp(by_source[k], -k, 0) for k in (1, 2, 3)]
    back = jnp.stack(back).reshape(8, 80, 1024)
    rows_back = jnp.concatenate(
        [
            lax.dynamic_index_in_dim(back, 2 * ((b // 2 - x) % 4) + ((b % 2) ^ z), 0, False)
            for b in range(8)
        ],
        axis=1,
    )
    upstream = rows_back[32:64]
    normed_rows = over_section(rows_back[:32], 1)
    sums = rows_back[64:70].astype(F32)
    whole = jnp.stack([sums[0] + sums[1] + sums[2], sums[3] + sums[4] + sums[5]])
    whole = whole + over_core(whole)
    whole = whole + sum(over_y(whole, k) for k in (1, 2, 3))
    whole = over_section(whole, 1)

    terms = [
        lax.dot_general(
            rows.reshape(256, 1024), weights, (((1,), (1,)), ((), ())), preferred_element_type=F32
        )
        .astype(BF)
        .reshape(8, 32, 1536)
        for rows in flowing
    ]
    term = {r: jnp.stack([t[place] for t in terms]) for place, r in enumerate(ORDER)}
    crossing = over_dp(term[(2, 1)], 0, 1).astype(F32)
    far = over_dp((term[(2, 0)].astype(F32) + crossing).astype(BF), -2, 0).astype(F32)
    other = term[(0, 1)].astype(F32)
    for k in (1, 3):
        other = other + over_dp(term[(k, 1)], -k, 0).astype(F32)
    context_sum = term[(0, 0)].astype(F32) + far
    for k in (1, 3):
        context_sum = context_sum + over_dp(term[(k, 0)], -k, 0).astype(F32)
    context_sum = context_sum + over_dp(other.astype(BF), 0, 1).astype(F32)
    context_sum = context_sum.astype(BF)
    kept, given = context_sum[..., :768], over_core(context_sum[..., 768:])
    both = jnp.stack([kept, given], axis=1)
    both = jnp.stack(
        [lax.dynamic_index_in_dim(both, (y - b) % 4, 0, False) for b in range(4)]
    )
    grad_context = jnp.where(core == 0, both, both[:, ::-1]).reshape(256, 768)

    spread = jnp.stack(flowing)
    weight_sum = sum(
        lax.dot_general(
            tokens[g], spread[:, 4 * g : 4 * g + 4], (((0, 1, 2), (0, 1, 2)), ((), ())), preferred_element_type=F32
        )
        for g in (0, 1)
    )
    grad_weight = weight_sum[:768] + over_core(weight_sum[768:].astype(BF)).astype(F32)
    return (
        normed_rows[None],
        upstream[None],
        grad_context[None],
        grad_weight[None],
        whole[0][None],
        whole[1][None],
    )


def solution(mesh):
    return jax.shard_map(
        shards,
        mesh=mesh,
        in_specs=(
            P("section", "dp", "mp"),
            P("section", ("dp", "mp"), None),
            P("section", "mp", "dp"),
            P("section", None),
            P("section", None),
            P("section", ("dp", "mp"), None),
        ),
        out_specs=(
            P("section", ("dp", "mp"), None),
            P("section", ("dp", "mp"), None),
            P("section", "dp", "mp"),
            P("section", "mp", "dp"),
            P("section", None),
            P("section", None),
        ),
        check_vma=False,
    )
```

```python
import jax
import jax.numpy as jnp
from jax import lax
from jax.experimental import pallas as pl
from jax.experimental.pallas import tpu as pltpu
from jax.sharding import PartitionSpec as P

EPSILON = 1e-05
WIDTH = 8192
BF = jnp.bfloat16
F32 = jnp.float32


def over_core(value):
    return lax.ppermute(value, "mp", [(i, i ^ 1) for i in range(8)])


def over_y(value, steps):
    return lax.ppermute(value, "mp", [(i, (i + 2 * steps) % 8) for i in range(8)])


def over_dp(value, steps, flip):
    return lax.ppermute(
        value, "dp", [(j, 2 * (((j >> 1) + steps) % 4) + ((j & 1) ^ flip)) for j in range(8)]
    )


def over_section(value, steps):
    return lax.ppermute(value, "section", [(s, (s + steps) % 2) for s in range(2)])


def over_both(value, steps, flip):
    pairs = [(i, (i + 8 * steps) % 16 ^ flip) for i in range(16)]
    return lax.ppermute(value, ("section", "dp"), pairs)


FIRST = ((0, 0), (0, 1), (1, 0), (3, 0))
SECOND = ((2, 0), (1, 1), (3, 1), (2, 1))
ORDER = FIRST + SECOND
NATURAL = tuple((k, f) for k in range(4) for f in range(2))


LANES = 128


def hidden_kernel(first, first_1, first_2, first_3, second, second_1, second_2, second_3, own, turned_1, turned_2, turned_3, gain, hidden, stats, stats_z):
    lane = lax.broadcasted_iota(jnp.int32, (32, LANES), 1)
    kind, place = lane // 32, lane % 8
    plain = jnp.zeros((32, LANES), F32)
    crossed = jnp.zeros((32, LANES), F32)
    turned = (own, turned_1, turned_2, turned_3)
    for index, (k, f) in enumerate(ORDER):
        group = (first, first_1, first_2, first_3) if index < 4 else (second, second_1, second_2, second_3)
        rows = pl.ds(index % 4 * 32, 32)
        attended = sum(part[rows, :].astype(F32) for part in group)
        value = (turned[k][f, 0].astype(F32) + attended).astype(BF)
        hidden[pl.ds(index * 32, 32), :] = value
        value = value.astype(F32)
        weighted = turned[k][f, 1].astype(F32) * gain[...]
        mean = jnp.sum(value, axis=-1, keepdims=True) * (1.0 / 1024)
        shifted = value - mean
        squares = jnp.sum(shifted * shifted, axis=-1, keepdims=True)
        total = jnp.sum(weighted, axis=-1, keepdims=True)
        cross = jnp.sum(weighted * shifted, axis=-1, keepdims=True)
        both = jnp.where(kind == 0, mean, jnp.where(kind == 1, squares, jnp.where(kind == 2, total, cross)))
        plain = jnp.where(place == 2 * k + f, both, plain)
        crossed = jnp.where(place == 2 * k + 1 - f, both, crossed)
    stats[...] = plain
    stats_z[...] = crossed


def norm_kernel(hidden, own, turned_1, turned_2, turned_3, gain, bias, stats, stats_1, stats_2, stats_3, returned, out, out_1, out_2, out_3):
    sets = [stats[0], stats[1]]
    for k, other in ((1, stats_1), (2, stats_2), (3, stats_3)):
        sets += [pltpu.roll(other[f], 2 * k, 1) for f in (0, 1)]
    added = sum(sets)
    mean = added * 0.125
    squares = pltpu.roll(added, LANES - 32, 1)
    total = pltpu.roll(added, LANES - 64, 1) * (1.0 / WIDTH)
    cross = pltpu.roll(added, LANES - 96, 1)
    for part in sets:
        apart = part - mean
        squares = squares + 1024.0 * apart * apart
        cross = cross + apart * pltpu.roll(part, LANES - 64, 1)
    scaled = lax.rsqrt(squares * (1.0 / WIDTH) + EPSILON)
    cross = cross * scaled * (1.0 / WIDTH)
    turned = (own, turned_1, turned_2, turned_3)
    outs = (out, out_1, out_2, out_3)
    gain_sum = jnp.zeros((1, 1024), F32)
    bias_sum = jnp.zeros((1, 1024), F32)
    for index, (k, f) in enumerate(ORDER):
        at = 8 + 2 * k + f
        rows = pl.ds(index * 32, 32)
        standard = (hidden[rows, :].astype(F32) - mean[:, at : at + 1]) * scaled[:, at : at + 1]
        incoming = turned[k][f, 1].astype(F32)
        weighted = incoming * gain[...]
        result = scaled[:, at : at + 1] * (weighted - total[:, at : at + 1] - standard * cross[:, at : at + 1])
        result = result.astype(BF)
        target = outs[k]
        returned[rows, :] = result
        target[f, 48:80, :] = result
        target[f, 0:32, :] = (standard * gain[...] + bias[...]).astype(BF)
        gain_sum = gain_sum + jnp.sum(incoming * standard, axis=0, keepdims=True)
        bias_sum = bias_sum + jnp.sum(incoming, axis=0, keepdims=True)
    row = lax.broadcasted_iota(jnp.int32, (16, 1024), 0)
    lines = jnp.zeros((16, 1024), F32)
    for first, rest in ((0, gain_sum), (3, bias_sum)):
        for place in range(3):
            part = rest.astype(BF).astype(F32)
            lines = jnp.where(row == first + place, part, lines)
            rest = rest - part
    lines = lines.astype(BF)
    for target in outs:
        target[0, 32:48, :] = lines
        target[1, 32:48, :] = lines


def called(kernel, results, *operands, flops=20_000_000):
    moved = sum(v.size * v.dtype.itemsize for v in (*operands, *results))
    return pl.pallas_call(
        kernel,
        out_shape=results,
        compiler_params=pltpu.CompilerParams(vmem_limit_bytes=32 * 2**20),
        cost_estimate=pl.CostEstimate(flops=flops, bytes_accessed=moved, transcendentals=4096),
    )(*operands)


def after(value, *others):
    return lax.optimization_barrier((value, *others))[0]


def shards(context, residual, out_weight, ln_gain, ln_bias, out_grad):
    mp, dp = lax.axis_index("mp"), lax.axis_index("dp")
    y, core = mp // 2, mp % 2
    x, z = dp // 2, dp % 2

    blocks = context[0].reshape(4, 2, 32, 768)
    by_y = [lax.dynamic_index_in_dim(blocks, (y - k) % 4, 0, False) for k in range(4)]
    theirs = jnp.stack([lax.dynamic_index_in_dim(b, 1 - core, 0, False) for b in by_y])
    mine = jnp.stack([lax.dynamic_index_in_dim(b, core, 0, False) for b in by_y])
    half = jnp.concatenate([mine, over_core(theirs)], axis=-1)

    sides = [
        [
            jnp.stack(
                [
                    lax.dynamic_slice_in_dim(rows[0], (2 * ((x + k) % 4) + side) * 1024, 1024, 1)
                    for k in range(4)
                ]
            )
            for side in (z, 1 - z)
        ]
        for rows in (residual, out_grad)
    ]
    stream = [sides[0][0], over_both(sides[0][1], 0, 1)]
    cotangent = [over_both(sides[1][f], -1, f) for f in (0, 1)]

    got = {(0, 0): half}
    got[(0, 1)] = over_dp(half, 0, 1)
    got[(3, 0)] = over_dp(half, 3, 0)
    got[(1, 0)] = over_dp(after(half, cotangent[1]), 1, 0)
    got[(2, 0)] = over_dp(after(half, cotangent[0], stream[1]), 2, 0)
    for k in (1, 3):
        got[(k, 1)] = over_dp(got[(0, 1)], k, 0)

    weight_own = out_weight[0]
    weight_other = over_core(after(weight_own, cotangent[1]))
    weights = jnp.concatenate([weight_own, weight_other], axis=0)
    got[(2, 1)] = over_dp(after(got[(2, 0)], weight_other), 0, 1)
    columns = jnp.concatenate(
        [
            lax.dynamic_slice_in_dim(ln_gain, dp * 1024, 1024, 1),
            lax.dynamic_slice_in_dim(ln_bias, dp * 1024, 1024, 1),
        ],
        axis=0,
    )
    columns = over_section(after(columns, got[(3, 0)]), -1)
    gain, bias = columns[:1], columns[1:]

    attended, tokens = [], []
    for group in (FIRST, SECOND):
        rows = jnp.stack([got[r] for r in group], axis=1)
        if attended:
            rows = after(rows, attended[0])
        tokens.append(rows)
        part = jnp.dot(rows.reshape(512, 1536), weights, preferred_element_type=F32).astype(BF)
        part = part.reshape(4, 128, 1024)
        attended += [part[0]] + [over_y(part[k], -k) for k in (1, 3, 2)]

    mixed = [jnp.stack([jnp.stack([stream[f][k], cotangent[f][k]]) for f in (0, 1)]) for k in range(4)]
    turned = [mixed[0]] + [over_dp(after(mixed[k], attended[0]), k, 0) for k in (1, 2, 3)]

    line = jax.ShapeDtypeStruct((32, LANES), F32)
    rows_here = jax.ShapeDtypeStruct((256, 1024), BF)
    hidden, stats, stats_z = called(
        hidden_kernel, (rows_here, line, line), *attended, *turned, gain
    )
    stats = jnp.stack([stats, over_dp(stats_z, 0, 1)])
    stats = [stats] + [over_dp(stats, k, 0) for k in (1, 2, 3)]
    block_out = jax.ShapeDtypeStruct((2, 80, 1024), BF)
    returned, *outs = called(
        norm_kernel, (rows_here, *[block_out] * 4), hidden, *turned, gain, bias, *stats
    )

    returned = returned.reshape(8, 32, 1024)
    flowing = [returned] + [over_y(returned, k) for k in (1, 2, 3)]

    crossed = [outs[0], over_dp(outs[1], -1, 0), None, over_dp(outs[3], -3, 0)]
    crossed[2] = over_dp(after(outs[2], crossed[1], crossed[3]), -2, 0)
    to_rows = lambda near, beside: jnp.concatenate(
        [
            jnp.where(b % 2 == z, *(lax.dynamic_index_in_dim(v, (b // 2 - x) % 4, 0, False) for v in (near, beside)))
            for b in range(8)
        ],
        axis=1,
    )
    gradient = [jnp.stack([c[f, 48:] for c in crossed]) for f in (0, 1)]
    ahead = [over_both(jnp.stack([c[f, :40] for c in crossed]), 1, f) for f in (0, 1)]
    upstream = to_rows(gradient[0], over_both(gradient[1], 0, 1))
    arrived = to_rows(*ahead)
    normed_rows = arrived[:32]
    sums = arrived[32:].astype(F32)
    whole = jnp.stack([sums[0] + sums[1] + sums[2], sums[3] + sums[4] + sums[5]])
    whole = whole + over_core(whole)
    whole = whole + sum(over_y(whole, k) for k in (1, 2, 3))

    flowing[1] = after(flowing[1], crossed[1], crossed[3])
    flowing[2] = after(flowing[2], crossed[2])
    terms = [
        lax.dot_general(
            rows.reshape(256, 1024), weights, (((1,), (1,)), ((), ())), preferred_element_type=F32
        )
        .astype(BF)
        .reshape(8, 32, 1536)
        for rows in flowing
    ]
    term = {r: jnp.stack([t[place] for t in terms]) for place, r in enumerate(ORDER)}
    crossing = over_dp(term[(2, 1)], 0, 1).astype(F32)
    near = [over_dp(jnp.stack([term[(k, 0)], term[(k, 1)]]), -k, 0).astype(F32) for k in (1, 3)]
    far = (term[(2, 0)].astype(F32) + crossing).astype(BF)
    far = over_dp(far, -2, 0).astype(F32)
    other = term[(0, 1)].astype(F32) + near[0][1] + near[1][1]
    other = over_dp(other.astype(BF), 0, 1).astype(F32)
    context_sum = (term[(0, 0)].astype(F32) + near[0][0] + near[1][0] + far + other).astype(BF)
    context_sum = after(context_sum, whole)
    kept, given = context_sum[..., :768], over_core(context_sum[..., 768:])
    both = jnp.stack([kept, given], axis=1)
    both = jnp.stack(
        [lax.dynamic_index_in_dim(both, (y - b) % 4, 0, False) for b in range(4)]
    )
    grad_context = jnp.where(core == 0, both, both[:, ::-1]).reshape(256, 768)

    spread = jnp.stack(flowing)
    weight_sum = sum(
        lax.dot_general(
            tokens[g], spread[:, 4 * g : 4 * g + 4], (((0, 1, 2), (0, 1, 2)), ((), ())), preferred_element_type=F32
        )
        for g in (0, 1)
    )
    grad_weight = weight_sum[:768] + over_core(weight_sum[768:].astype(BF)).astype(F32)
    return (
        normed_rows[None],
        upstream[None],
        grad_context[None],
        grad_weight[None],
        whole[0][None],
        whole[1][None],
    )


def solution(mesh):
    return jax.shard_map(
        shards,
        mesh=mesh,
        in_specs=(
            P("section", "dp", "mp"),
            P("section", ("dp", "mp"), None),
            P("section", "mp", "dp"),
            P("section", None),
            P("section", None),
            P("section", ("dp", "mp"), None),
        ),
        out_specs=(
            P("section", ("dp", "mp"), None),
            P("section", ("dp", "mp"), None),
            P("section", "dp", "mp"),
            P("section", "mp", "dp"),
            P("section", None),
            P("section", None),
        ),
        check_vma=False,
    )
```

```python
import jax
import jax.numpy as jnp
from jax import lax
from jax.experimental import pallas as pl
from jax.experimental.pallas import tpu as pltpu
from jax.sharding import PartitionSpec as P

EPSILON = 1e-05
WIDTH = 8192
BF = jnp.bfloat16
F32 = jnp.float32


def over_core(value):
    return lax.ppermute(value, "mp", [(i, i ^ 1) for i in range(8)])


def over_y(value, steps):
    return lax.ppermute(value, "mp", [(i, (i + 2 * steps) % 8) for i in range(8)])


def over_dp(value, steps, flip):
    return lax.ppermute(
        value, "dp", [(j, 2 * (((j >> 1) + steps) % 4) + ((j & 1) ^ flip)) for j in range(8)]
    )


def over_section(value, steps):
    return lax.ppermute(value, "section", [(s, (s + steps) % 2) for s in range(2)])


def over_both(value, steps, flip):
    pairs = [(i, (i + 8 * steps) % 16 ^ flip) for i in range(16)]
    return lax.ppermute(value, ("section", "dp"), pairs)


FIRST = ((0, 0), (0, 1), (1, 0), (3, 0))
SECOND = ((2, 0), (1, 1), (3, 1), (2, 1))
ORDER = FIRST + SECOND
NATURAL = tuple((k, f) for k in range(4) for f in range(2))


LANES = 128


def hidden_kernel(first, first_1, first_2, first_3, second, second_1, second_2, second_3, own, turned_1, turned_2, turned_3, gain, hidden, stats, stats_z):
    lane = lax.broadcasted_iota(jnp.int32, (32, LANES), 1)
    kind, place = lane // 32, lane % 8
    plain = jnp.zeros((32, LANES), F32)
    crossed = jnp.zeros((32, LANES), F32)
    turned = (own, turned_1, turned_2, turned_3)
    for index, (k, f) in enumerate(ORDER):
        group = (first, first_1, first_2, first_3) if index < 4 else (second, second_1, second_2, second_3)
        rows = pl.ds(index % 4 * 32, 32)
        attended = sum(part[rows, :].astype(F32) for part in group)
        value = (turned[k][f, 0].astype(F32) + attended).astype(BF)
        hidden[pl.ds(index * 32, 32), :] = value
        value = value.astype(F32)
        weighted = turned[k][f, 1].astype(F32) * gain[...]
        mean = jnp.sum(value, axis=-1, keepdims=True) * (1.0 / 1024)
        shifted = value - mean
        squares = jnp.sum(shifted * shifted, axis=-1, keepdims=True)
        total = jnp.sum(weighted, axis=-1, keepdims=True)
        cross = jnp.sum(weighted * shifted, axis=-1, keepdims=True)
        both = jnp.where(kind == 0, mean, jnp.where(kind == 1, squares, jnp.where(kind == 2, total, cross)))
        plain = jnp.where(place == 2 * k + f, both, plain)
        crossed = jnp.where(place == 2 * k + 1 - f, both, crossed)
    stats[...] = plain
    stats_z[...] = crossed


def norm_kernel(hidden, own, turned_1, turned_2, turned_3, gain, bias, stats, stats_1, stats_2, stats_3, returned, out, out_1, out_2, out_3):
    sets = [stats[0], stats[1]]
    for k, other in ((1, stats_1), (2, stats_2), (3, stats_3)):
        sets += [pltpu.roll(other[f], 2 * k, 1) for f in (0, 1)]
    added = sum(sets)
    mean = added * 0.125
    squares = pltpu.roll(added, LANES - 32, 1)
    total = pltpu.roll(added, LANES - 64, 1) * (1.0 / WIDTH)
    cross = pltpu.roll(added, LANES - 96, 1)
    for part in sets:
        apart = part - mean
        squares = squares + 1024.0 * apart * apart
        cross = cross + apart * pltpu.roll(part, LANES - 64, 1)
    scaled = lax.rsqrt(squares * (1.0 / WIDTH) + EPSILON)
    cross = cross * scaled * (1.0 / WIDTH)
    turned = (own, turned_1, turned_2, turned_3)
    outs = (out, out_1, out_2, out_3)
    gain_sum = jnp.zeros((1, 1024), F32)
    bias_sum = jnp.zeros((1, 1024), F32)
    for index, (k, f) in enumerate(ORDER):
        at = 8 + 2 * k + f
        rows = pl.ds(index * 32, 32)
        standard = (hidden[rows, :].astype(F32) - mean[:, at : at + 1]) * scaled[:, at : at + 1]
        incoming = turned[k][f, 1].astype(F32)
        weighted = incoming * gain[...]
        result = scaled[:, at : at + 1] * (weighted - total[:, at : at + 1] - standard * cross[:, at : at + 1])
        result = result.astype(BF)
        target = outs[k]
        returned[rows, :] = result
        target[f, 48:80, :] = result
        target[f, 0:32, :] = (standard * gain[...] + bias[...]).astype(BF)
        gain_sum = gain_sum + jnp.sum(incoming * standard, axis=0, keepdims=True)
        bias_sum = bias_sum + jnp.sum(incoming, axis=0, keepdims=True)
    row = lax.broadcasted_iota(jnp.int32, (16, 1024), 0)
    lines = jnp.zeros((16, 1024), F32)
    for first, rest in ((0, gain_sum), (3, bias_sum)):
        for place in range(3):
            part = rest.astype(BF).astype(F32)
            lines = jnp.where(row == first + place, part, lines)
            rest = rest - part
    lines = lines.astype(BF)
    for target in outs:
        target[0, 32:48, :] = lines
        target[1, 32:48, :] = lines


def called(kernel, results, *operands, flops=20_000_000):
    moved = sum(v.size * v.dtype.itemsize for v in (*operands, *results))
    return pl.pallas_call(
        kernel,
        out_shape=results,
        compiler_params=pltpu.CompilerParams(vmem_limit_bytes=32 * 2**20),
        cost_estimate=pl.CostEstimate(flops=flops, bytes_accessed=moved, transcendentals=4096),
    )(*operands)


def after(value, *others):
    return lax.optimization_barrier((value, *others))[0]


def shards(context, residual, out_weight, ln_gain, ln_bias, out_grad):
    mp, dp = lax.axis_index("mp"), lax.axis_index("dp")
    y, core = mp // 2, mp % 2
    x, z = dp // 2, dp % 2

    blocks = context[0].reshape(4, 2, 32, 768)
    by_y = [lax.dynamic_index_in_dim(blocks, (y - k) % 4, 0, False) for k in range(4)]
    theirs = jnp.stack([lax.dynamic_index_in_dim(b, 1 - core, 0, False) for b in by_y])
    mine = jnp.stack([lax.dynamic_index_in_dim(b, core, 0, False) for b in by_y])
    half = jnp.concatenate([mine, over_core(theirs)], axis=-1)

    sides = [
        [
            jnp.stack(
                [
                    lax.dynamic_slice_in_dim(rows[0], (2 * ((x + k) % 4) + side) * 1024, 1024, 1)
                    for k in range(4)
                ]
            )
            for side in (z, 1 - z)
        ]
        for rows in (residual, out_grad)
    ]
    stream = [sides[0][0], over_both(after(sides[0][1], half), 0, 1)]
    cotangent = [over_both(after(sides[1][f], half), -1, f) for f in (0, 1)]

    got = {(0, 0): half}
    got[(0, 1)] = over_dp(half, 0, 1)
    got[(3, 0)] = over_dp(half, 3, 0)
    got[(1, 0)] = over_dp(half, 1, 0)
    got[(2, 0)] = over_dp(after(half, *cotangent, stream[1]), 2, 0)
    for k in (1, 3):
        got[(k, 1)] = over_dp(got[(0, 1)], k, 0)

    weight_own = out_weight[0]
    weight_other = over_core(after(weight_own, cotangent[1]))
    weights = jnp.concatenate([weight_own, weight_other], axis=0)
    got[(2, 1)] = over_dp(after(got[(2, 0)], weight_other), 0, 1)
    columns = jnp.concatenate(
        [
            lax.dynamic_slice_in_dim(ln_gain, dp * 1024, 1024, 1),
            lax.dynamic_slice_in_dim(ln_bias, dp * 1024, 1024, 1),
        ],
        axis=0,
    )
    columns = over_section(after(columns, got[(3, 0)]), -1)
    gain, bias = columns[:1], columns[1:]

    attended, tokens = [], []
    for group in (FIRST, SECOND):
        rows = jnp.stack([got[r] for r in group], axis=1)
        if attended:
            rows = after(rows, attended[0])
        tokens.append(rows)
        part = jnp.dot(rows.reshape(512, 1536), weights, preferred_element_type=F32).astype(BF)
        part = part.reshape(4, 128, 1024)
        attended += [part[0]] + [over_y(part[k], -k) for k in (1, 3, 2)]

    mixed = [jnp.stack([jnp.stack([stream[f][k], cotangent[f][k]]) for f in (0, 1)]) for k in range(4)]
    turned = [mixed[0]] + [over_dp(after(mixed[k], attended[0]), k, 0) for k in (1, 2, 3)]

    line = jax.ShapeDtypeStruct((32, LANES), F32)
    rows_here = jax.ShapeDtypeStruct((256, 1024), BF)
    hidden, stats, stats_z = called(
        hidden_kernel, (rows_here, line, line), *attended, *turned, gain
    )
    stats = jnp.stack([stats, over_dp(stats_z, 0, 1)])
    stats = [stats] + [over_dp(stats, k, 0) for k in (1, 2, 3)]
    block_out = jax.ShapeDtypeStruct((2, 80, 1024), BF)
    returned, *outs = called(
        norm_kernel, (rows_here, *[block_out] * 4), hidden, *turned, gain, bias, *stats
    )

    returned = returned.reshape(8, 32, 1024)
    flowing = [returned] + [over_y(returned, k) for k in (1, 2, 3)]

    crossed = [outs[0], over_dp(outs[1], -1, 0), None, over_dp(outs[3], -3, 0)]
    crossed[2] = over_dp(after(outs[2], crossed[1], crossed[3]), -2, 0)
    to_rows = lambda near, beside: jnp.concatenate(
        [
            jnp.where(b % 2 == z, *(lax.dynamic_index_in_dim(v, (b // 2 - x) % 4, 0, False) for v in (near, beside)))
            for b in range(8)
        ],
        axis=1,
    )
    gradient = [jnp.stack([c[f, 48:] for c in crossed]) for f in (0, 1)]
    ahead = [over_both(jnp.stack([c[f, :40] for c in crossed]), 1, f) for f in (0, 1)]
    arrived = to_rows(*ahead)
    normed_rows = arrived[:32]
    sums = arrived[32:].astype(F32)
    whole = jnp.stack([sums[0] + sums[1] + sums[2], sums[3] + sums[4] + sums[5]])
    whole = whole + over_core(whole)
    whole = whole + sum(over_y(whole, k) for k in (1, 2, 3))

    flowing[1] = after(flowing[1], crossed[1], crossed[3])
    flowing[2] = after(flowing[2], crossed[2])
    terms = [
        lax.dot_general(
            rows.reshape(256, 1024), weights, (((1,), (1,)), ((), ())), preferred_element_type=F32
        )
        .astype(BF)
        .reshape(8, 32, 1536)
        for rows in flowing
    ]
    term = {r: jnp.stack([t[place] for t in terms]) for place, r in enumerate(ORDER)}
    passing = over_dp(term[(2, 1)], 0, 1)
    crossing = passing.astype(F32)
    near = [over_dp(jnp.stack([term[(k, 0)], term[(k, 1)]]), -k, 0).astype(F32) for k in (1, 3)]
    far = (term[(2, 0)].astype(F32) + crossing).astype(BF)
    far = over_dp(far, -2, 0).astype(F32)
    upstream = to_rows(gradient[0], over_both(after(gradient[1], passing), 0, 1))
    other = term[(0, 1)].astype(F32) + near[0][1] + near[1][1]
    other = over_dp(other.astype(BF), 0, 1).astype(F32)
    spread = jnp.stack(flowing)
    weight_sum = sum(
        lax.dot_general(
            tokens[g], spread[:, 4 * g : 4 * g + 4], (((0, 1, 2), (0, 1, 2)), ((), ())), preferred_element_type=F32
        )
        for g in (0, 1)
    )
    grad_weight = weight_sum[:768] + over_core(after(weight_sum[768:].astype(BF), passing)).astype(F32)
    here = after(term[(0, 0)].astype(F32) + near[0][0] + near[1][0], grad_weight)
    context_sum = (here + far + other).astype(BF)
    kept, given = context_sum[..., :768], over_core(context_sum[..., 768:])
    both = jnp.stack([kept, given], axis=1)
    both = jnp.stack(
        [lax.dynamic_index_in_dim(both, (y - b) % 4, 0, False) for b in range(4)]
    )
    grad_context = jnp.where(core == 0, both, both[:, ::-1]).reshape(256, 768)

    return (
        normed_rows[None],
        upstream[None],
        grad_context[None],
        grad_weight[None],
        whole[0][None],
        whole[1][None],
    )


def solution(mesh):
    return jax.shard_map(
        shards,
        mesh=mesh,
        in_specs=(
            P("section", "dp", "mp"),
            P("section", ("dp", "mp"), None),
            P("section", "mp", "dp"),
            P("section", None),
            P("section", None),
            P("section", ("dp", "mp"), None),
        ),
        out_specs=(
            P("section", ("dp", "mp"), None),
            P("section", ("dp", "mp"), None),
            P("section", "dp", "mp"),
            P("section", "mp", "dp"),
            P("section", None),
            P("section", None),
        ),
        check_vma=False,
    )
```

```python
import jax
import jax.numpy as jnp
from jax import lax
from jax.experimental import pallas as pl
from jax.experimental.pallas import tpu as pltpu
from jax.sharding import PartitionSpec as P

EPSILON = 1e-05
WIDTH = 8192
BF = jnp.bfloat16
F32 = jnp.float32


def over_core(value):
    return lax.ppermute(value, "mp", [(i, i ^ 1) for i in range(8)])


def over_y(value, steps):
    return lax.ppermute(value, "mp", [(i, (i + 2 * steps) % 8) for i in range(8)])


def over_dp(value, steps, flip):
    return lax.ppermute(
        value, "dp", [(j, 2 * (((j >> 1) + steps) % 4) + ((j & 1) ^ flip)) for j in range(8)]
    )


def over_section(value, steps):
    return lax.ppermute(value, "section", [(s, (s + steps) % 2) for s in range(2)])


def over_both(value, steps, flip):
    pairs = [(i, (i + 8 * steps) % 16 ^ flip) for i in range(16)]
    return lax.ppermute(value, ("section", "dp"), pairs)


FIRST = ((0, 0), (0, 1), (1, 0), (3, 0))
SECOND = ((2, 0), (1, 1), (3, 1), (2, 1))
ORDER = FIRST + SECOND
NATURAL = tuple((k, f) for k in range(4) for f in range(2))


LANES = 128


def hidden_kernel(first, first_1, first_2, first_3, second, second_1, second_2, second_3, own, turned_1, turned_2, turned_3, gain, hidden, stats, stats_z):
    lane = lax.broadcasted_iota(jnp.int32, (32, LANES), 1)
    kind, place = lane // 32, lane % 8
    plain = jnp.zeros((32, LANES), F32)
    crossed = jnp.zeros((32, LANES), F32)
    turned = (own, turned_1, turned_2, turned_3)
    for index, (k, f) in enumerate(ORDER):
        group = (first, first_1, first_2, first_3) if index < 4 else (second, second_1, second_2, second_3)
        rows = pl.ds(index % 4 * 32, 32)
        attended = sum(part[rows, :].astype(F32) for part in group)
        value = (turned[k][f, 0].astype(F32) + attended).astype(BF)
        hidden[pl.ds(index * 32, 32), :] = value
        value = value.astype(F32)
        weighted = turned[k][f, 1].astype(F32) * gain[...]
        mean = jnp.sum(value, axis=-1, keepdims=True) * (1.0 / 1024)
        shifted = value - mean
        squares = jnp.sum(shifted * shifted, axis=-1, keepdims=True)
        total = jnp.sum(weighted, axis=-1, keepdims=True)
        cross = jnp.sum(weighted * shifted, axis=-1, keepdims=True)
        both = jnp.where(kind == 0, mean, jnp.where(kind == 1, squares, jnp.where(kind == 2, total, cross)))
        plain = jnp.where(place == 2 * k + f, both, plain)
        crossed = jnp.where(place == 2 * k + 1 - f, both, crossed)
    stats[...] = plain
    stats_z[...] = crossed


def norm_kernel(hidden, own, turned_1, turned_2, turned_3, gain, bias, stats, stats_1, stats_2, stats_3, returned, out, out_1, out_2, out_3):
    sets = [stats[0], stats[1]]
    for k, other in ((1, stats_1), (2, stats_2), (3, stats_3)):
        sets += [pltpu.roll(other[f], 2 * k, 1) for f in (0, 1)]
    added = sum(sets)
    mean = added * 0.125
    squares = pltpu.roll(added, LANES - 32, 1)
    total = pltpu.roll(added, LANES - 64, 1) * (1.0 / WIDTH)
    cross = pltpu.roll(added, LANES - 96, 1)
    for part in sets:
        apart = part - mean
        squares = squares + 1024.0 * apart * apart
        cross = cross + apart * pltpu.roll(part, LANES - 64, 1)
    scaled = lax.rsqrt(squares * (1.0 / WIDTH) + EPSILON)
    cross = cross * scaled * (1.0 / WIDTH)
    turned = (own, turned_1, turned_2, turned_3)
    outs = (out, out_1, out_2, out_3)
    gain_sum = jnp.zeros((1, 1024), F32)
    bias_sum = jnp.zeros((1, 1024), F32)
    for index, (k, f) in enumerate(ORDER):
        at = 8 + 2 * k + f
        rows = pl.ds(index * 32, 32)
        standard = (hidden[rows, :].astype(F32) - mean[:, at : at + 1]) * scaled[:, at : at + 1]
        incoming = turned[k][f, 1].astype(F32)
        weighted = incoming * gain[...]
        result = scaled[:, at : at + 1] * (weighted - total[:, at : at + 1] - standard * cross[:, at : at + 1])
        result = result.astype(BF)
        target = outs[k]
        returned[rows, :] = result
        target[f, 48:80, :] = result
        target[f, 0:32, :] = (standard * gain[...] + bias[...]).astype(BF)
        gain_sum = gain_sum + jnp.sum(incoming * standard, axis=0, keepdims=True)
        bias_sum = bias_sum + jnp.sum(incoming, axis=0, keepdims=True)
    row = lax.broadcasted_iota(jnp.int32, (16, 1024), 0)
    lines = jnp.zeros((16, 1024), F32)
    for first, rest in ((0, gain_sum), (3, bias_sum)):
        for place in range(3):
            part = rest.astype(BF).astype(F32)
            lines = jnp.where(row == first + place, part, lines)
            rest = rest - part
    lines = lines.astype(BF)
    for target in outs:
        target[0, 32:48, :] = lines
        target[1, 32:48, :] = lines


def called(kernel, results, *operands, flops=20_000_000):
    moved = sum(v.size * v.dtype.itemsize for v in (*operands, *results))
    return pl.pallas_call(
        kernel,
        out_shape=results,
        compiler_params=pltpu.CompilerParams(vmem_limit_bytes=32 * 2**20),
        cost_estimate=pl.CostEstimate(flops=flops, bytes_accessed=moved, transcendentals=4096),
    )(*operands)


def after(value, *others):
    return lax.optimization_barrier((value, *others))[0]


def shards(context, residual, out_weight, ln_gain, ln_bias, out_grad):
    mp, dp = lax.axis_index("mp"), lax.axis_index("dp")
    y, core = mp // 2, mp % 2
    x, z = dp // 2, dp % 2

    blocks = context[0].reshape(4, 2, 32, 768)
    by_y = [lax.dynamic_index_in_dim(blocks, (y - k) % 4, 0, False) for k in range(4)]
    theirs = jnp.stack([lax.dynamic_index_in_dim(b, 1 - core, 0, False) for b in by_y])
    mine = jnp.stack([lax.dynamic_index_in_dim(b, core, 0, False) for b in by_y])
    half = jnp.concatenate([mine, over_core(theirs)], axis=-1)

    sides = [
        [
            jnp.stack(
                [
                    lax.dynamic_slice_in_dim(rows[0], (2 * ((x + k) % 4) + side) * 1024, 1024, 1)
                    for k in range(4)
                ]
            )
            for side in (z, 1 - z)
        ]
        for rows in (residual, out_grad)
    ]
    stream = [sides[0][0], over_both(after(sides[0][1], half), 0, 1)]
    cotangent = [over_both(after(sides[1][f], half), -1, f) for f in (0, 1)]

    got = {(0, 0): half}
    got[(0, 1)] = over_dp(half, 0, 1)
    got[(3, 0)] = over_dp(half, 3, 0)
    got[(1, 0)] = over_dp(half, 1, 0)
    got[(2, 0)] = over_dp(after(half, *cotangent, stream[1]), 2, 0)
    for k in (1, 3):
        got[(k, 1)] = over_dp(got[(0, 1)], k, 0)

    weight_own = out_weight[0]
    weight_other = over_core(after(weight_own, cotangent[1]))
    weights = jnp.concatenate([weight_own, weight_other], axis=0)
    columns = jnp.concatenate(
        [
            lax.dynamic_slice_in_dim(ln_gain, dp * 1024, 1024, 1),
            lax.dynamic_slice_in_dim(ln_bias, dp * 1024, 1024, 1),
        ],
        axis=0,
    )
    columns = over_section(after(columns, got[(3, 0)]), -1)
    got[(2, 1)] = over_dp(after(got[(2, 0)], weight_other, columns), 0, 1)
    gain, bias = columns[:1], columns[1:]

    attended, tokens = [], []
    for group in (FIRST, SECOND):
        rows = jnp.stack([got[r] for r in group], axis=1)
        if attended:
            rows = after(rows, attended[0])
        tokens.append(rows)
        part = jnp.dot(rows.reshape(512, 1536), weights, preferred_element_type=F32).astype(BF)
        part = part.reshape(4, 128, 1024)
        attended += [part[0]] + [over_y(part[k], -k) for k in (1, 3, 2)]

    mixed = [jnp.stack([jnp.stack([stream[f][k], cotangent[f][k]]) for f in (0, 1)]) for k in range(4)]
    turned = [mixed[0]] + [over_dp(after(mixed[k], attended[4]), k, 0) for k in (1, 2, 3)]

    line = jax.ShapeDtypeStruct((32, LANES), F32)
    rows_here = jax.ShapeDtypeStruct((256, 1024), BF)
    hidden, stats, stats_z = called(
        hidden_kernel, (rows_here, line, line), *attended, *turned, gain
    )
    stats = jnp.stack([stats, over_dp(stats_z, 0, 1)])
    stats = [stats] + [over_dp(stats, k, 0) for k in (1, 2, 3)]
    block_out = jax.ShapeDtypeStruct((2, 80, 1024), BF)
    returned, *outs = called(
        norm_kernel, (rows_here, *[block_out] * 4), hidden, *turned, gain, bias, *stats
    )

    returned = returned.reshape(8, 32, 1024)
    flowing = [returned] + [over_y(returned, k) for k in (1, 2, 3)]

    crossed = [outs[0], over_dp(outs[1], -1, 0), None, over_dp(outs[3], -3, 0)]
    crossed[2] = over_dp(after(outs[2], crossed[1], crossed[3]), -2, 0)
    to_rows = lambda near, beside: jnp.concatenate(
        [
            jnp.where(b % 2 == z, *(lax.dynamic_index_in_dim(v, (b // 2 - x) % 4, 0, False) for v in (near, beside)))
            for b in range(8)
        ],
        axis=1,
    )
    gradient = [jnp.stack([c[f, 48:] for c in crossed]) for f in (0, 1)]
    ahead = [over_both(jnp.stack([c[f, :40] for c in crossed]), 1, f) for f in (0, 1)]
    arrived = to_rows(*ahead)
    normed_rows = arrived[:32]
    sums = arrived[32:].astype(F32)
    whole = jnp.stack([sums[0] + sums[1] + sums[2], sums[3] + sums[4] + sums[5]])
    whole = whole + over_core(whole)
    whole = whole + sum(over_y(whole, k) for k in (1, 2, 3))

    flowing[1] = after(flowing[1], crossed[1], crossed[3])
    flowing[2] = after(flowing[2], crossed[2])
    terms = [
        lax.dot_general(
            rows.reshape(256, 1024), weights, (((1,), (1,)), ((), ())), preferred_element_type=F32
        )
        .astype(BF)
        .reshape(8, 32, 1536)
        for rows in flowing
    ]
    term = {r: jnp.stack([t[place] for t in terms]) for place, r in enumerate(ORDER)}
    passing = over_dp(term[(2, 1)], 0, 1)
    crossing = passing.astype(F32)
    near = [over_dp(jnp.stack([term[(k, 0)], term[(k, 1)]]), -k, 0).astype(F32) for k in (1, 3)]
    far = (term[(2, 0)].astype(F32) + crossing).astype(BF)
    far = over_dp(far, -2, 0).astype(F32)
    upstream = to_rows(gradient[0], after(over_both(after(gradient[1], passing), 0, 1), near[0], near[1]))
    other = term[(0, 1)].astype(F32) + near[0][1] + near[1][1]
    other = over_dp(other.astype(BF), 0, 1).astype(F32)
    spread = jnp.stack(flowing)
    weight_sum = sum(
        lax.dot_general(
            tokens[g], spread[:, 4 * g : 4 * g + 4], (((0, 1, 2), (0, 1, 2)), ((), ())), preferred_element_type=F32
        )
        for g in (0, 1)
    )
    grad_weight = weight_sum[:768] + over_core(after(weight_sum[768:].astype(BF), passing)).astype(F32)
    here = after(term[(0, 0)].astype(F32) + near[0][0] + near[1][0], grad_weight)
    context_sum = (here + far + other).astype(BF)
    kept, given = context_sum[..., :768], over_core(context_sum[..., 768:])
    both = jnp.stack([kept, given], axis=1)
    both = jnp.stack(
        [lax.dynamic_index_in_dim(both, (y - b) % 4, 0, False) for b in range(4)]
    )
    grad_context = jnp.where(core == 0, both, both[:, ::-1]).reshape(256, 768)

    return (
        normed_rows[None],
        upstream[None],
        grad_context[None],
        grad_weight[None],
        whole[0][None],
        whole[1][None],
    )


def solution(mesh):
    return jax.shard_map(
        shards,
        mesh=mesh,
        in_specs=(
            P("section", "dp", "mp"),
            P("section", ("dp", "mp"), None),
            P("section", "mp", "dp"),
            P("section", None),
            P("section", None),
            P("section", ("dp", "mp"), None),
        ),
        out_specs=(
            P("section", ("dp", "mp"), None),
            P("section", ("dp", "mp"), None),
            P("section", "dp", "mp"),
            P("section", "mp", "dp"),
            P("section", None),
            P("section", None),
        ),
        check_vma=False,
    )
```

```python
import jax
import jax.numpy as jnp
from jax import lax
from jax.experimental import pallas as pl
from jax.experimental.pallas import tpu as pltpu
from jax.sharding import PartitionSpec as P

EPSILON = 1e-05
WIDTH = 8192
BF = jnp.bfloat16
F32 = jnp.float32


def over_core(value):
    return lax.ppermute(value, "mp", [(i, i ^ 1) for i in range(8)])


def over_y(value, steps):
    return lax.ppermute(value, "mp", [(i, (i + 2 * steps) % 8) for i in range(8)])


def over_dp(value, steps, flip):
    return lax.ppermute(
        value, "dp", [(j, 2 * (((j >> 1) + steps) % 4) + ((j & 1) ^ flip)) for j in range(8)]
    )


def over_section(value, steps):
    return lax.ppermute(value, "section", [(s, (s + steps) % 2) for s in range(2)])


def over_both(value, steps, flip):
    pairs = [(i, (i + 8 * steps) % 16 ^ flip) for i in range(16)]
    return lax.ppermute(value, ("section", "dp"), pairs)


FIRST = ((0, 0), (0, 1), (1, 0), (3, 0))
SECOND = ((2, 0), (1, 1), (3, 1), (2, 1))
ORDER = FIRST + SECOND
NATURAL = tuple((k, f) for k in range(4) for f in range(2))


LANES = 128


def hidden_kernel(first, first_1, first_2, first_3, second, second_1, second_2, second_3, own, turned_1, turned_2, turned_3, gain, hidden, stats, stats_z):
    lane = lax.broadcasted_iota(jnp.int32, (32, LANES), 1)
    kind, place = lane // 32, lane % 8
    plain = jnp.zeros((32, LANES), F32)
    crossed = jnp.zeros((32, LANES), F32)
    turned = (own, turned_1, turned_2, turned_3)
    for index, (k, f) in enumerate(ORDER):
        group = (first, first_1, first_2, first_3) if index < 4 else (second, second_1, second_2, second_3)
        rows = pl.ds(index % 4 * 32, 32)
        attended = sum(part[rows, :].astype(F32) for part in group)
        value = (turned[k][f, 0].astype(F32) + attended).astype(BF)
        hidden[pl.ds(index * 32, 32), :] = value
        value = value.astype(F32)
        weighted = turned[k][f, 1].astype(F32) * gain[...]
        mean = jnp.sum(value, axis=-1, keepdims=True) * (1.0 / 1024)
        shifted = value - mean
        squares = jnp.sum(shifted * shifted, axis=-1, keepdims=True)
        total = jnp.sum(weighted, axis=-1, keepdims=True)
        cross = jnp.sum(weighted * shifted, axis=-1, keepdims=True)
        both = jnp.where(kind == 0, mean, jnp.where(kind == 1, squares, jnp.where(kind == 2, total, cross)))
        plain = jnp.where(place == 2 * k + f, both, plain)
        crossed = jnp.where(place == 2 * k + 1 - f, both, crossed)
    stats[...] = plain
    stats_z[...] = crossed


def norm_kernel(hidden, own, turned_1, turned_2, turned_3, gain, bias, stats, stats_1, stats_2, stats_3, returned, out, out_1, out_2, out_3):
    sets = [stats[0], stats[1]]
    for k, other in ((1, stats_1), (2, stats_2), (3, stats_3)):
        sets += [pltpu.roll(other[f], 2 * k, 1) for f in (0, 1)]
    added = sum(sets)
    mean = added * 0.125
    squares = pltpu.roll(added, LANES - 32, 1)
    total = pltpu.roll(added, LANES - 64, 1) * (1.0 / WIDTH)
    cross = pltpu.roll(added, LANES - 96, 1)
    for part in sets:
        apart = part - mean
        squares = squares + 1024.0 * apart * apart
        cross = cross + apart * pltpu.roll(part, LANES - 64, 1)
    scaled = lax.rsqrt(squares * (1.0 / WIDTH) + EPSILON)
    cross = cross * scaled * (1.0 / WIDTH)
    turned = (own, turned_1, turned_2, turned_3)
    outs = (out, out_1, out_2, out_3)
    gain_sum = jnp.zeros((1, 1024), F32)
    bias_sum = jnp.zeros((1, 1024), F32)
    for index, (k, f) in enumerate(ORDER):
        at = 8 + 2 * k + f
        rows = pl.ds(index * 32, 32)
        standard = (hidden[rows, :].astype(F32) - mean[:, at : at + 1]) * scaled[:, at : at + 1]
        incoming = turned[k][f, 1].astype(F32)
        weighted = incoming * gain[...]
        result = scaled[:, at : at + 1] * (weighted - total[:, at : at + 1] - standard * cross[:, at : at + 1])
        result = result.astype(BF)
        target = outs[k]
        returned[rows, :] = result
        target[f, 48:80, :] = result
        target[f, 0:32, :] = (standard * gain[...] + bias[...]).astype(BF)
        gain_sum = gain_sum + jnp.sum(incoming * standard, axis=0, keepdims=True)
        bias_sum = bias_sum + jnp.sum(incoming, axis=0, keepdims=True)
    row = lax.broadcasted_iota(jnp.int32, (16, 1024), 0)
    lines = jnp.zeros((16, 1024), F32)
    for first, rest in ((0, gain_sum), (3, bias_sum)):
        for place in range(3):
            part = rest.astype(BF).astype(F32)
            lines = jnp.where(row == first + place, part, lines)
            rest = rest - part
    lines = lines.astype(BF)
    for target in outs:
        target[0, 32:48, :] = lines
        target[1, 32:48, :] = lines


def called(kernel, results, *operands, flops=20_000_000):
    moved = sum(v.size * v.dtype.itemsize for v in (*operands, *results))
    return pl.pallas_call(
        kernel,
        out_shape=results,
        compiler_params=pltpu.CompilerParams(vmem_limit_bytes=32 * 2**20),
        cost_estimate=pl.CostEstimate(flops=flops, bytes_accessed=moved, transcendentals=4096),
    )(*operands)


def after(value, *others):
    return lax.optimization_barrier((value, *others))[0]


def shards(context, residual, out_weight, ln_gain, ln_bias, out_grad):
    mp, dp = lax.axis_index("mp"), lax.axis_index("dp")
    y, core = mp // 2, mp % 2
    x, z = dp // 2, dp % 2

    blocks = context[0].reshape(4, 2, 32, 768)
    by_y = [lax.dynamic_index_in_dim(blocks, (y - k) % 4, 0, False) for k in range(4)]
    theirs = jnp.stack([lax.dynamic_index_in_dim(b, 1 - core, 0, False) for b in by_y])
    mine = jnp.stack([lax.dynamic_index_in_dim(b, core, 0, False) for b in by_y])
    half = jnp.concatenate([mine, over_core(theirs)], axis=-1)

    sides = [
        [
            jnp.stack(
                [
                    lax.dynamic_slice_in_dim(rows[0], (2 * ((x + k) % 4) + side) * 1024, 1024, 1)
                    for k in range(4)
                ]
            )
            for side in (z, 1 - z)
        ]
        for rows in (residual, out_grad)
    ]
    stream = [sides[0][0], None]
    cotangent = [over_both(after(sides[1][f], half), -1, f) for f in (0, 1)]

    got = {(0, 0): half}
    got[(0, 1)] = over_dp(half, 0, 1)
    stream[1] = over_both(after(sides[0][1], got[(0, 1)]), 0, 1)
    got[(3, 0)] = over_dp(half, 3, 0)
    got[(1, 0)] = over_dp(half, 1, 0)
    got[(2, 0)] = over_dp(after(half, cotangent[0]), 2, 0)
    for k in (1, 3):
        got[(k, 1)] = over_dp(got[(0, 1)], k, 0)

    weight_own = out_weight[0]
    weight_other = over_core(after(weight_own, cotangent[1]))
    weights = jnp.concatenate([weight_own, weight_other], axis=0)
    columns = jnp.concatenate(
        [
            lax.dynamic_slice_in_dim(ln_gain, dp * 1024, 1024, 1),
            lax.dynamic_slice_in_dim(ln_bias, dp * 1024, 1024, 1),
        ],
        axis=0,
    )
    columns = over_section(after(columns, got[(3, 0)]), -1)
    got[(2, 1)] = over_dp(after(got[(2, 0)], weight_other, columns), 0, 1)
    gain, bias = columns[:1], columns[1:]

    attended, tokens = [], []
    for group in (FIRST, SECOND):
        rows = jnp.stack([got[r] for r in group], axis=1)
        if attended:
            rows = after(rows, attended[0])
        tokens.append(rows)
        part = jnp.dot(rows.reshape(512, 1536), weights, preferred_element_type=F32).astype(BF)
        part = part.reshape(4, 128, 1024)
        attended += [part[0]] + [over_y(part[k], -k) for k in (1, 3, 2)]

    mixed = [jnp.stack([jnp.stack([stream[f][k], cotangent[f][k]]) for f in (0, 1)]) for k in range(4)]
    turned = [mixed[0]] + [over_dp(after(mixed[k], attended[4]), k, 0) for k in (1, 2, 3)]

    line = jax.ShapeDtypeStruct((32, LANES), F32)
    rows_here = jax.ShapeDtypeStruct((256, 1024), BF)
    hidden, stats, stats_z = called(
        hidden_kernel, (rows_here, line, line), *attended, *turned, gain
    )
    stats = jnp.stack([stats, over_dp(stats_z, 0, 1)])
    stats = [stats] + [over_dp(stats, k, 0) for k in (1, 2, 3)]
    block_out = jax.ShapeDtypeStruct((2, 80, 1024), BF)
    returned, *outs = called(
        norm_kernel, (rows_here, *[block_out] * 4), hidden, *turned, gain, bias, *stats
    )

    returned = returned.reshape(8, 32, 1024)
    flowing = [returned] + [over_y(returned, k) for k in (1, 2, 3)]

    crossed = [outs[0], over_dp(outs[1], -1, 0), None, over_dp(outs[3], -3, 0)]
    crossed[2] = over_dp(after(outs[2], crossed[1], crossed[3]), -2, 0)
    to_rows = lambda near, beside: jnp.concatenate(
        [
            jnp.where(b % 2 == z, *(lax.dynamic_index_in_dim(v, (b // 2 - x) % 4, 0, False) for v in (near, beside)))
            for b in range(8)
        ],
        axis=1,
    )
    gradient = [jnp.stack([c[f, 48:] for c in crossed]) for f in (0, 1)]
    ahead = [over_both(jnp.stack([c[f, :40] for c in crossed]), 1, f) for f in (0, 1)]
    arrived = to_rows(*ahead)
    normed_rows = arrived[:32]
    sums = arrived[32:].astype(F32)
    whole = jnp.stack([sums[0] + sums[1] + sums[2], sums[3] + sums[4] + sums[5]])
    whole = whole + over_core(whole)
    whole = whole + sum(over_y(whole, k) for k in (1, 2, 3))

    flowing[1] = after(flowing[1], crossed[1], crossed[3])
    flowing[2] = after(flowing[2], crossed[2])
    terms = [
        lax.dot_general(
            rows.reshape(256, 1024), weights, (((1,), (1,)), ((), ())), preferred_element_type=F32
        )
        .astype(BF)
        .reshape(8, 32, 1536)
        for rows in flowing
    ]
    term = {r: jnp.stack([t[place] for t in terms]) for place, r in enumerate(ORDER)}
    passing = over_dp(term[(2, 1)], 0, 1)
    crossing = passing.astype(F32)
    near = [over_dp(jnp.stack([term[(k, 0)], term[(k, 1)]]), -k, 0).astype(F32) for k in (1, 3)]
    far = (term[(2, 0)].astype(F32) + crossing).astype(BF)
    far = over_dp(far, -2, 0).astype(F32)
    aside = over_both(after(gradient[1], passing), 0, 1)
    other = term[(0, 1)].astype(F32) + near[0][1] + near[1][1]
    other = over_dp(other.astype(BF), 0, 1).astype(F32)
    spread = jnp.stack(flowing)
    weight_sum = sum(
        lax.dot_general(
            tokens[g], spread[:, 4 * g : 4 * g + 4], (((0, 1, 2), (0, 1, 2)), ((), ())), preferred_element_type=F32
        )
        for g in (0, 1)
    )
    grad_weight = weight_sum[:768] + over_core(after(weight_sum[768:].astype(BF), passing)).astype(F32)
    here = after(term[(0, 0)].astype(F32) + near[0][0] + near[1][0], grad_weight)
    context_sum = (here + far + other).astype(BF)
    upstream = to_rows(gradient[0], after(aside, context_sum))
    kept, given = context_sum[..., :768], over_core(context_sum[..., 768:])
    both = jnp.stack([kept, given], axis=1)
    both = jnp.stack(
        [lax.dynamic_index_in_dim(both, (y - b) % 4, 0, False) for b in range(4)]
    )
    grad_context = jnp.where(core == 0, both, both[:, ::-1]).reshape(256, 768)

    return (
        normed_rows[None],
        upstream[None],
        grad_context[None],
        grad_weight[None],
        whole[0][None],
        whole[1][None],
    )


def solution(mesh):
    return jax.shard_map(
        shards,
        mesh=mesh,
        in_specs=(
            P("section", "dp", "mp"),
            P("section", ("dp", "mp"), None),
            P("section", "mp", "dp"),
            P("section", None),
            P("section", None),
            P("section", ("dp", "mp"), None),
        ),
        out_specs=(
            P("section", ("dp", "mp"), None),
            P("section", ("dp", "mp"), None),
            P("section", "dp", "mp"),
            P("section", "mp", "dp"),
            P("section", None),
            P("section", None),
        ),
        check_vma=False,
    )
```
